128 devices in a mesh: head: 4 (over x), frame: 32 (over y, z, core).
Axes of the slice: x: 4, y: 4, z: 4, core: 2. Of those that a mesh axis runs over, the one named last changes fastest.
Arguments:
- frames_x: bfloat16 [16384, 3072], P('frame'), may hold values from -6 to 6
- w_qkv: bfloat16 [3072, 9216], P(None, 'head'), may hold values from -0.109375 to 0.109375
- q_gain: float32 [128], replicated, may hold values from 0.5 to 2.5
- k_gain: float32 [128], replicated, may hold values from 0.5 to 2.5
- head_kind: int32 [24], P('head'), may hold values from 0 to 1, as said below
- w_out: bfloat16 [3072, 3072], P('head'), may hold values from -0.109375 to 0.109375
Outputs:
- mixed: bfloat16 [16384, 3072], P('frame', 'head')
The draws below stay inside these ranges and needn't reach their ends.
Inputs may be any that keep to these rules, and one draw needn't show every extreme that they name: `head_kind`: in each group of 6 consecutive heads, 1 to 4 heads are temporal; some group has exactly 4.
All inputs are finite; a program needn't handle non-finite values.
Results may differ from the reference program's by a relative error of at most 0.015.
Values may be sent and summed in bfloat16 or wider, within the bound.
A program may use at most 192 MiB of HBM per device.

```python
import math
import jax
import jax.numpy as jnp
from jax import lax

HEADS = 24
HD = 128
TOK_F = 512
TMAX = 4
D = 3072
GROUPS = 4
HPG = 6
FRAMES = 32
TOKENS = 16384


def draw_head_kind(key, part):
    key = jax.random.fold_in(key, 7)
    first_key, second_key, third_key = jax.random.split(key, 3)
    counts = jax.random.randint(first_key, (GROUPS,), 1, TMAX + 1)
    fullest = jax.random.randint(second_key, (), 0, GROUPS)
    counts = jnp.where(jnp.arange(GROUPS) == fullest, TMAX, counts)
    noise = jax.random.randint(third_key, (GROUPS, HPG), 0, 2 ** 20)
    order = jnp.argsort(noise * HPG + jnp.arange(HPG)[None, :], axis=1)
    ranks = jnp.argsort(order, axis=1)
    kinds = (ranks < counts[:, None]).astype(jnp.int32)
    return kinds.reshape(HEADS)


def steps_of(own_key, dims, pieces, smallest, largest):
    def one(position, shards_of):
        steps = jax.random.uniform(jax.random.fold_in(jax.random.fold_in(own_key, 6), position), (shards_of,), jnp.float32, smallest / len(pieces), largest / len(pieces))
        return jnp.repeat(jnp.exp(steps), dims[position] // shards_of).reshape((-1,) + (1,) * (len(dims) - position - 1))

    level = one(*pieces[0])
    for cut in pieces[1:]:
        level = level * one(*cut)
    return level


def centred(stream_key, extent, width, bound, cuts=(), dtype=jnp.bfloat16):
    entries = width * jax.random.normal(stream_key, extent, jnp.float32)
    if cuts:
        entries = entries * steps_of(stream_key, extent, cuts, -0.22, 0.18)
    return jnp.clip(entries, -bound, bound).astype(dtype)


def setup_inputs(seed: int = 0) -> dict:
    key_list = jax.random.split(jax.random.key(seed), 7)
    return {
        "frames_x": centred(key_list[0], (TOKENS, D), 1.0, 6.0, ((0, 32),)),
        "w_qkv": centred(key_list[1], (D, HEADS * 3 * HD), D ** -0.5, 0.109375, ((1, 4),)),
        "q_gain": jnp.clip(jnp.exp(jax.random.uniform(key_list[2], (HD,), jnp.float32, math.log(0.5), math.log(2.5))), 0.5, 2.5),
        "k_gain": jnp.clip(jnp.exp(jax.random.uniform(key_list[3], (HD,), jnp.float32, math.log(0.5), math.log(2.5))), 0.5, 2.5),
        "head_kind": draw_head_kind(jax.random.fold_in(key_list[6], 71), 0),
        "w_out": centred(key_list[5], (HEADS * HD, D), (HEADS * HD) ** -0.5, 0.109375, ((0, 4),)),
    }


EPSILON = 1e-06

def rms_norm(values, gains):
    mean_square = lax.optimization_barrier(jnp.mean(values * values, axis=-1, keepdims=True))
    return values * lax.rsqrt(mean_square + EPSILON) * gains

def softmax_rows(scores):
    shifted = scores - lax.optimization_barrier(jnp.max(scores, axis=-1, keepdims=True))
    weights = jnp.exp(shifted)
    return weights / lax.optimization_barrier(jnp.sum(weights, axis=-1, keepdims=True))

def round_half(values):
    rounded = lax.optimization_barrier(values.astype(jnp.bfloat16))
    return rounded.astype(jnp.float32)

def reference(frames_x, w_qkv, q_gain, k_gain, head_kind, w_out):
    scale = 1.0 / math.sqrt(HD)
    projected = jnp.dot(frames_x, w_qkv, preferred_element_type=jnp.float32)
    projected = projected.reshape(FRAMES, TOK_F, HEADS, 3, HD)
    queries = rms_norm(projected[:, :, :, 0], q_gain.astype(jnp.float32)).astype(jnp.bfloat16)
    keys = rms_norm(projected[:, :, :, 1], k_gain.astype(jnp.float32)).astype(jnp.bfloat16)
    values = projected[:, :, :, 2].astype(jnp.bfloat16)

    def one_head(operands):
        query, key, value, kind = operands
        query_f = query.astype(jnp.float32)
        key_f = key.astype(jnp.float32)
        value_f = value.astype(jnp.float32)
        wide_keys = jnp.concatenate([key_f, jnp.broadcast_to(key_f[:1], key_f.shape)], axis=1)
        wide_values = jnp.concatenate([value_f, jnp.broadcast_to(value_f[:1], value_f.shape)], axis=1)
        spatial_scores = jnp.einsum('ftd,fsd->fts', query_f, wide_keys) * scale
        spatial_probs = round_half(softmax_rows(spatial_scores))
        spatial = jnp.einsum('fts,fsd->ftd', spatial_probs, wide_values).astype(jnp.bfloat16)
        temporal_scores = jnp.einsum('ftd,gtd->tfg', query_f, key_f) * scale
        temporal_probs = round_half(softmax_rows(temporal_scores))
        temporal = jnp.einsum('tfg,gtd->ftd', temporal_probs, value_f).astype(jnp.bfloat16)
        return jnp.where(kind == 1, temporal, spatial)
    heads_first = lax.map(one_head, (jnp.moveaxis(queries, 2, 0), jnp.moveaxis(keys, 2, 0), jnp.moveaxis(values, 2, 0), head_kind))
    attention = jnp.moveaxis(heads_first, 0, 2).reshape(FRAMES * TOK_F, HEADS * HD)
    group_width = HPG * HD
    total = jnp.zeros((FRAMES * TOK_F, HEADS * HD), jnp.float32)
    for group in range(GROUPS):
        lower = group * group_width
        group_part = jnp.dot(attention[:, lower:lower + group_width], w_out[lower:lower + group_width], preferred_element_type=jnp.float32).astype(jnp.bfloat16)
        total = total + group_part.astype(jnp.float32)
    return total.astype(jnp.bfloat16)
```

```python
import functools
import math

import jax
import jax.numpy as jnp
from jax import lax
from jax.experimental import pallas as pl
from jax.experimental.pallas import tpu as pltpu
from jax.sharding import PartitionSpec as P

MESH = pl.DeviceIdType.MESH
EPSILON = 1e-06
HPG = 6
TMAX = 4
HD = 128
TOK = 512
D = 3072
WAVES = 4
WT = TOK // WAVES
COLS = D // 4
HALF = WT // 2
BF = jnp.bfloat16
F32 = jnp.float32


def dot(a, b):
    return jnp.dot(a, b, preferred_element_type=F32)


def dot_t(a, b):
    return lax.dot_general(a, b, (((1,), (1,)), ((), ())), preferred_element_type=F32)


def arrived(ref, sem):
    pltpu.make_async_copy(ref, ref, sem).wait()


def kernel(
    kinds, x_hbm, w_hbm, qg_ref, kg_ref, wo_hbm, out_ref,
    x, w, wo, qkv, kv0, sbuf, rbuf, obuf, tbuf, perm, unperm, sp, att,
    far_s, far_r, near_s, near_r,
    load_sem, a2a_s, a2a_r, ret_s, ret_r, sc_s, sc_r, st_s, st_r, fs_sem, fr_sem, ns_sem, nr_sem,
):
    nf = 32
    h = lax.axis_index("head")
    f = lax.axis_index("frame")
    core = lax.rem(f, 2)
    chip = f // 2
    y, z = chip // 4, lax.rem(chip, 4)
    left, right, opposite = lax.rem(h + 3, 4), lax.rem(h + 1, 4), lax.rem(h + 2, 4)

    barrier = pltpu.get_barrier_semaphore()

    @pl.loop(1, nf)
    def _(i):
        pl.semaphore_signal(barrier, inc=1, device_id=(h, lax.rem(f + i, nf)), device_id_type=MESH)

    for peer in (left, right):
        pl.semaphore_signal(barrier, inc=1, device_id=(peer, f), device_id_type=MESH)

    loads = [pltpu.make_async_copy(x_hbm, x, load_sem.at[0])]
    for c in range(3):
        loads.append(
            pltpu.make_async_copy(w_hbm.at[:, pl.ds(768 * c, 768)], w.at[c], load_sem.at[1 + c])
        )
    for b in range(4):
        loads.append(
            pltpu.make_async_copy(wo_hbm.at[:, pl.ds(COLS * b, COLS)], wo.at[b], load_sem.at[4 + b])
        )
    for load in loads:
        load.start()

    kind = [kinds[j] for j in range(HPG)]
    count = sum(kind)
    holds = [[None] * HPG for _ in range(TMAX)]
    before = jnp.int32(0)
    for j in range(HPG):
        rank = kind[j] * before + (1 - kind[j]) * (count + j - before)
        for t in range(TMAX):
            holds[t][j] = (1 - jnp.minimum((rank - t) * (rank - t), 1)).astype(F32)
        before = before + kind[j]
    kind = [val.astype(F32) for val in kind]

    def spread(shape, mixed_dim):
        mixed = lax.broadcasted_iota(jnp.int32, shape, mixed_dim)
        token = lax.broadcasted_iota(jnp.int32, shape, 1 - mixed_dim)
        same = ((mixed // 16) * 4 + mixed % 4 == token).astype(F32)
        slot = (mixed // 4) % 4
        return [jnp.where(slot == t, same, 0.0) for t in range(TMAX)]

    slots = spread((TOK, WT), 0)
    for j in range(HPG):
        perm[:, WT * j : WT * j + WT] = sum(slots[t] * holds[t][j] for t in range(TMAX)).astype(BF)
    slots = spread((WT, TOK), 1)
    for j in range(HPG):
        total = sum(slots[t] * (holds[t][j] * kind[j]) for t in range(TMAX))
        unperm[WT * j : WT * j + WT] = total.astype(BF)
    for j in range(HPG):
        qkv[j, :, 3 * HD :] = jnp.ones((TOK, HD), BF)
        kv0[j, :, 2 * HD :] = jnp.ones((TOK, HD), BF)
    for v in range(WAVES):
        rbuf[v, :, 3 * HD :] = jnp.ones((TOK, HD), BF)

    q_gain = qg_ref[...] * (math.log2(math.e) / math.sqrt(HD))
    k_gain = kg_ref[...]

    def norm(val, gain):
        mean_square = jnp.mean(val * val, axis=-1, keepdims=True)
        return (val * lax.rsqrt(mean_square + EPSILON) * gain).astype(BF)

    def project(c):
        loads[1 + c].wait()
        for part in range(3):
            val = dot(x[...], w[c, :, 256 * part : 256 * part + 256])
            for side in range(2):
                piece = 2 * part + side
                head, role = 2 * c + piece // 3, piece % 3
                block = val[:, HD * side : HD * side + HD]
                if role == 0:
                    block = norm(block, q_gain)
                elif role == 1:
                    block = norm(block, k_gain)
                else:
                    block = block.astype(BF)
                qkv[head, :, HD * role : HD * role + HD] = block

    batches = ((0, 4, True), (4, 2, False))

    def cut(batch, start, size):
        lo, n, _ = batches[batch]
        return kv0.at[pl.ds(lo, n), pl.ds(start, size), pl.ds(0, 2 * HD)]

    def device_of(yy, zz):
        return (yy * 4 + zz) * 2

    def scatter(batch):
        lo, n, z_first = batches[batch]

        @pl.when(f == 0)
        def _():
            kv0[lo : lo + n, :, : 2 * HD] = qkv[lo : lo + n, :, HD : 3 * HD]

            @pl.loop(1, 16)
            def _(q):
                major, minor = q // 4, lax.rem(q, 4)
                target = device_of(major, minor) if z_first else device_of(minor, major)
                piece = cut(batch, pl.multiple_of(q * 32, 32), 32)
                pltpu.make_async_remote_copy(
                    src_ref=piece, dst_ref=piece, send_sem=sc_s.at[batch], recv_sem=sc_r.at[batch],
                    device_id=(h, target), device_id_type=MESH,
                ).start()

    def peers_copy(batch, stage, start, size, along_z):
        for i in range(1, 4):
            if along_z:
                target = device_of(y, lax.rem(z + i, 4))
            else:
                target = device_of(lax.rem(y + i, 4), z)
            piece = cut(batch, start, size)

            @pl.when(target != 0)
            def _():
                pltpu.make_async_remote_copy(
                    src_ref=piece, dst_ref=piece, send_sem=st_s.at[batch, stage], recv_sem=st_r.at[batch, stage],
                    device_id=(h, target), device_id_type=MESH,
                ).start()

    def stage(batch, number):
        z_first = batches[batch][2]
        major, minor = (y, z) if z_first else (z, y)

        @pl.when(core == 0)
        def _():
            if number == 0:
                @pl.when(f != 0)
                def _():
                    arrived(cut(batch, 0, 32), sc_r.at[batch])

                peers_copy(batch, 0, pl.multiple_of((major * 4 + minor) * 32, 32), 32, z_first)
            elif number == 1:
                @pl.when(f != 0)
                def _():
                    arrived(cut(batch, 0, 96), st_r.at[batch, 0])

                peers_copy(batch, 1, pl.multiple_of(major * 128, 128), 128, not z_first)
            else:
                @pl.when(f != 0)
                def _():
                    arrived(cut(batch, 0, 384), st_r.at[batch, 1])

                piece = cut(batch, 0, TOK)
                pltpu.make_async_remote_copy(
                    src_ref=piece, dst_ref=piece, send_sem=st_s.at[batch, 2], recv_sem=st_r.at[batch, 2],
                    device_id=(h, f + 1), device_id_type=MESH,
                ).start()

    def stages_done(batch):
        @pl.when(core == 1)
        def _():
            arrived(cut(batch, 0, TOK), st_r.at[batch, 2])

    def stages_sent(batch):
        @pl.when(f == 0)
        def _():
            arrived(cut(batch, 0, 480), sc_s.at[batch])

        @pl.when(core == 0)
        def _():
            for number, size in ((0, 32), (1, 128)):
                along_z = batches[batch][2] == (number == 0)
                on_line = ((y == 0) & (z != 0)) if along_z else ((z == 0) & (y != 0))

                @pl.when(on_line)
                def _():
                    arrived(cut(batch, 0, 2 * size), st_s.at[batch, number])

                @pl.when(jnp.logical_not(on_line))
                def _():
                    arrived(cut(batch, 0, 3 * size), st_s.at[batch, number])

            arrived(cut(batch, 0, TOK), st_s.at[batch, 2])

    def send_wave(v):
        picked = jnp.concatenate(
            [qkv[j, WT * v : WT * v + WT, : 3 * HD] for j in range(HPG)], axis=0
        )
        sbuf[v] = dot(perm[...], picked).astype(BF)

        @pl.loop(1, nf)
        def _(i):
            p = lax.rem(f + i, nf)
            pltpu.make_async_remote_copy(
                src_ref=sbuf.at[v, pl.ds(pl.multiple_of(p * 16, 16), 16)],
                dst_ref=rbuf.at[v, pl.ds(pl.multiple_of(f * 16, 16), 16), pl.ds(0, 3 * HD)],
                send_sem=a2a_s.at[v], recv_sem=a2a_r.at[v], device_id=(h, p), device_id_type=MESH,
            ).start()

        own = pl.ds(pl.multiple_of(f * 16, 16), 16)
        rbuf[v, own, : 3 * HD] = sbuf[v, own]

    def attend(scores, vals):
        return dot(jnp.exp2(scores).astype(BF), vals)

    def close(total):
        return (total[:, :HD] / total[:, HD:]).astype(BF)

    def temporal(v):
        arrived(rbuf.at[v, pl.ds(0, 496), pl.ds(0, 3 * HD)], a2a_r.at[v])
        scores = dot_t(rbuf[v, :, :HD], rbuf[v, :, HD : 2 * HD])
        same = (lax.broadcasted_iota(jnp.int32, (TOK, TOK), 0) % 16) == (
            lax.broadcasted_iota(jnp.int32, (TOK, TOK), 1) % 16
        )
        weights = jnp.where(same, jnp.exp2(scores), 0.0).astype(BF)
        obuf[v] = close(dot(weights, rbuf[v, :, 2 * HD :]))

        @pl.loop(1, nf)
        def _(i):
            p = lax.rem(f + i, nf)
            pltpu.make_async_remote_copy(
                src_ref=obuf.at[v, pl.ds(pl.multiple_of(p * 16, 16), 16)],
                dst_ref=tbuf.at[v, pl.ds(pl.multiple_of(f * 16, 16), 16)],
                send_sem=ret_s.at[v], recv_sem=ret_r.at[v], device_id=(h, p), device_id_type=MESH,
            ).start()

        own = pl.ds(pl.multiple_of(f * 16, 16), 16)
        tbuf[v, own] = obuf[v, own]

    def spatial(j):
        query = qkv[j, :, :HD]
        total = attend(dot_t(query, qkv[j, :, HD : 2 * HD]), qkv[j, :, 2 * HD :])
        total = total + attend(dot_t(query, kv0[j, :, :HD]), kv0[j, :, HD:])
        sp[j] = close(total)

    def copy_to(src, dst, send_sem, recv_sem, peer):
        return pltpu.make_async_remote_copy(
            src_ref=src, dst_ref=dst, send_sem=send_sem, recv_sem=recv_sem,
            device_id=(peer, f), device_id_type=MESH,
        )

    def far_copies(v):
        return (
            copy_to(far_s.at[v, 0], far_r.at[v, 0], fs_sem.at[v, 0], fr_sem.at[v, 0], left),
            copy_to(far_s.at[v, 1], far_r.at[v, 1], fs_sem.at[v, 1], fr_sem.at[v, 1], right),
        )

    def near_copies(v):
        return (
            copy_to(near_s.at[v, 0], near_r.at[v, 0], ns_sem.at[v, 0], nr_sem.at[v, 0], left),
            copy_to(near_s.at[v, 1], near_r.at[v, 1], ns_sem.at[v, 1], nr_sem.at[v, 1], right),
        )

    def project_out(v):
        rows = slice(WT * v, WT * v + WT)
        arrived(tbuf.at[v, pl.ds(0, 496)], ret_r.at[v])
        back = dot(unperm[...], tbuf[v])
        for j in range(HPG):
            block = back[WT * j : WT * j + WT] + sp[j, rows].astype(F32) * (1.0 - kind[j])
            att[rows, HD * j : HD * j + HD] = block.astype(BF)
        part = dot(att[rows], wo[opposite]).astype(BF)
        far_s[v, 0] = part[:HALF]
        far_s[v, 1] = part[HALF:]
        for copy in far_copies(v):
            copy.start()

    def reduce_near(v):
        rows = slice(WT * v, WT * v + WT)
        far = far_copies(v)
        near = near_copies(v)
        part = dot(att[rows], wo[left])
        far[0].wait_recv()
        near_s[v, 0, :HALF] = (part[:HALF] + far_r[v, 0].astype(F32)).astype(BF)
        near_s[v, 0, HALF:] = part[HALF:].astype(BF)
        near[0].start()
        part = dot(att[rows], wo[right])
        far[1].wait_recv()
        near_s[v, 1, :HALF] = part[:HALF].astype(BF)
        near_s[v, 1, HALF:] = (part[HALF:] + far_r[v, 1].astype(F32)).astype(BF)
        near[1].start()

    def finish(v):
        rows = slice(WT * v, WT * v + WT)
        near = near_copies(v)
        part = dot(att[rows], wo[h]).astype(BF).astype(F32)
        near[0].wait_recv()
        near[1].wait_recv()
        out_ref[rows] = (part + near_r[v, 0].astype(F32) + near_r[v, 1].astype(F32)).astype(BF)

    loads[0].wait()
    project(0)
    pl.semaphore_wait(barrier, nf + 1)
    project(1)
    scatter(0)
    project(2)
    scatter(1)
    send_wave(0)
    stage(0, 0)
    send_wave(1)
    stage(0, 1)
    stage(1, 0)
    for b in range(4):
        loads[4 + b].wait()
    stage(0, 2)
    stage(1, 1)
    send_wave(2)
    stage(1, 2)
    temporal(0)
    send_wave(3)
    stages_done(0)
    stages_done(1)
    for j in range(HPG):
        spatial(j)
    project_out(0)
    temporal(1)
    reduce_near(0)
    project_out(1)
    temporal(2)
    reduce_near(1)
    project_out(2)
    temporal(3)
    reduce_near(2)
    finish(0)
    project_out(3)
    reduce_near(3)
    finish(1)
    finish(2)
    finish(3)

    stages_sent(0)
    stages_sent(1)
    for v in range(WAVES):
        arrived(sbuf.at[v, pl.ds(0, 496)], a2a_s.at[v])
        arrived(obuf.at[v, pl.ds(0, 496)], ret_s.at[v])
        for copy in far_copies(v) + near_copies(v):
            copy.wait_send()


def per_device(frames_x, w_qkv, q_gain, k_gain, head_kind, w_out):
    any_spec = pl.BlockSpec(memory_space=pl.ANY)
    vmem = pl.BlockSpec(memory_space=pltpu.VMEM)
    dma = pltpu.SemaphoreType.DMA
    return pl.pallas_call(
        kernel,
        out_shape=jax.ShapeDtypeStruct((TOK, COLS), BF),
        in_specs=[pl.BlockSpec(memory_space=pltpu.SMEM), any_spec, any_spec, vmem, vmem, any_spec],
        out_specs=vmem,
        scratch_shapes=[
            pltpu.VMEM((TOK, D), BF),
            pltpu.VMEM((3, D, 768), BF),
            pltpu.VMEM((4, HPG * HD, COLS), BF),
            pltpu.VMEM((HPG, TOK, 4 * HD), BF),
            pltpu.VMEM((HPG, TOK, 3 * HD), BF),
            pltpu.VMEM((WAVES, TOK, 3 * HD), BF),
            pltpu.VMEM((WAVES, TOK, 4 * HD), BF),
            pltpu.VMEM((WAVES, TOK, HD), BF),
            pltpu.VMEM((WAVES, TOK, HD), BF),
            pltpu.VMEM((TOK, HPG * WT), BF),
            pltpu.VMEM((HPG * WT, TOK), BF),
            pltpu.VMEM((HPG, TOK, HD), BF),
            pltpu.VMEM((TOK, HPG * HD), BF),
            pltpu.VMEM((WAVES, 2, HALF, COLS), BF),
            pltpu.VMEM((WAVES, 2, HALF, COLS), BF),
            pltpu.VMEM((WAVES, 2, WT, COLS), BF),
            pltpu.VMEM((WAVES, 2, WT, COLS), BF),
            dma((8,)),
            dma((WAVES,)),
            dma((WAVES,)),
            dma((WAVES,)),
            dma((WAVES,)),
            dma((2,)),
            dma((2,)),
            dma((2, 3)),
            dma((2, 3)),
            dma((WAVES, 2)),
            dma((WAVES, 2)),
            dma((WAVES, 2)),
            dma((WAVES, 2)),
        ],
        compiler_params=pltpu.CompilerParams(
            collective_id=0, has_side_effects=True, vmem_limit_bytes=60 * 1024 * 1024
        ),
    )(head_kind, frames_x, w_qkv, q_gain.reshape(1, HD), k_gain.reshape(1, HD), w_out)


def solution(mesh):
    placed = (P("frame", None), P(None, "head"), P(), P(), P("head"), P("head", None))
    return jax.shard_map(
        per_device, mesh=mesh, in_specs=placed, out_specs=P("frame", "head"), check_vma=False
    )
```

```python
import functools
import math

import jax
import jax.numpy as jnp
from jax import lax
from jax.experimental import pallas as pl
from jax.experimental.pallas import tpu as pltpu
from jax.sharding import PartitionSpec as P

MESH = pl.DeviceIdType.MESH
EPSILON = 1e-06
HPG = 6
TMAX = 4
HD = 128
TOK = 512
D = 3072
WAVES = 4
WT = TOK // WAVES
COLS = D // 4
CHUNKS = 9
SECTIONS = ((0,), (1, 2), (3, 4, 5), (6, 7, 8))
STARTS = (4, 6, 9, 12, 14)
HALF = WT // 2
WIDE = COLS // 2
BATCH = 2
BATCHES = HPG // BATCH
BF = jnp.bfloat16
F32 = jnp.float32


def dot(a, b):
    return jnp.dot(a, b, preferred_element_type=F32)


def dot_t(a, b):
    return lax.dot_general(a, b, (((1,), (1,)), ((), ())), preferred_element_type=F32)


def arrived(ref, sem):
    pltpu.make_async_copy(ref, ref, sem).wait()


def kernel(
    kinds, x_hbm, w_hbm, qg_ref, kg_ref, wo_hbm, out_ref,
    x, w, wo, raw, qkv, kv0, sbuf, rbuf, obuf, tbuf, perm, unperm, sp, att,
    far_s, far_r, near_s, near_r,
    load_sem, a2a_s, a2a_r, ret_s, ret_r, sc_s, sc_r, st_s, st_r, co_s, co_r, fs_sem, fr_sem, ns_sem, nr_sem,
):
    nf = 32
    h = lax.axis_index("head")
    f = lax.axis_index("frame")
    core = lax.rem(f, 2)
    chip = f // 2
    left, right, opposite = lax.rem(h + 3, 4), lax.rem(h + 1, 4), lax.rem(h + 2, 4)

    barrier = pltpu.get_barrier_semaphore()

    @pl.loop(1, nf)
    def _(i):
        pl.semaphore_signal(barrier, inc=1, device_id=(h, lax.rem(f + i, nf)), device_id_type=MESH)

    for peer in (left, right):
        pl.semaphore_signal(barrier, inc=1, device_id=(peer, f), device_id_type=MESH)

    loads = [pltpu.make_async_copy(x_hbm, x, load_sem.at[0])]
    for c in range(CHUNKS):
        loads.append(
            pltpu.make_async_copy(w_hbm.at[:, pl.ds(256 * c, 256)], w.at[c], load_sem.at[1 + c])
        )
    for b in range(4):
        loads.append(
            pltpu.make_async_copy(wo_hbm.at[:, pl.ds(COLS * b, COLS)], wo.at[b], load_sem.at[10 + b])
        )
    for load in loads[: STARTS[0]]:
        load.start()

    kind = [kinds[j] for j in range(HPG)]
    count = sum(kind)
    holds = [[None] * HPG for _ in range(TMAX)]
    before = jnp.int32(0)
    for j in range(HPG):
        rank = kind[j] * before + (1 - kind[j]) * (count + j - before)
        for t in range(TMAX):
            holds[t][j] = (1 - jnp.minimum((rank - t) * (rank - t), 1)).astype(F32)
        before = before + kind[j]
    kind = [val.astype(F32) for val in kind]

    def spread(shape, mixed_dim):
        mixed = lax.broadcasted_iota(jnp.int32, shape, mixed_dim)
        token = lax.broadcasted_iota(jnp.int32, shape, 1 - mixed_dim)
        same = ((mixed // 16) * 4 + mixed % 4 == token).astype(F32)
        slot = (mixed // 4) % 4
        return [jnp.where(slot == t, same, 0.0) for t in range(TMAX)]

    slots = spread((TOK, WT), 0)
    for j in range(HPG):
        perm[:, WT * j : WT * j + WT] = sum(slots[t] * holds[t][j] for t in range(TMAX)).astype(BF)
    slots = spread((WT, TOK), 1)
    for j in range(HPG):
        total = sum(slots[t] * (holds[t][j] * kind[j]) for t in range(TMAX))
        unperm[WT * j : WT * j + WT] = total.astype(BF)
    for j in range(HPG):
        qkv[j, :, 3 * HD :] = jnp.ones((TOK, HD), BF)
        kv0[j, :, 2 * HD :] = jnp.ones((TOK, HD), BF)
    for v in range(WAVES):
        rbuf[v, :, 3 * HD :] = jnp.ones((TOK, HD), BF)

    q_gain = qg_ref[...] * (math.log2(math.e) / math.sqrt(HD))
    k_gain = kg_ref[...]

    def norm(val, gain):
        mean_square = jnp.mean(val * val, axis=-1, keepdims=True)
        return (val * lax.rsqrt(mean_square + EPSILON) * gain).astype(BF)

    def project(number):
        for c in SECTIONS[number]:
            loads[1 + c].wait()
        for load in loads[STARTS[number] : STARTS[number + 1]]:
            load.start()
        for i, c in enumerate(SECTIONS[number]):
            raw[number % 2, :, 256 * i : 256 * i + 256] = dot(x[...], w[c])

    def settle(number):
        for piece in range(2 * SECTIONS[number][0], 2 * SECTIONS[number][-1] + 2):
            head, role = piece // 3, piece % 3
            at = HD * (piece - 2 * SECTIONS[number][0])
            block = raw[number % 2, :, at : at + HD]
            if role == 0:
                block = norm(block, q_gain)
            elif role == 1:
                block = norm(block, k_gain)
            else:
                block = block.astype(BF)
            qkv[head, :, HD * role : HD * role + HD] = block

    def cut(batch, start, size, own=False):
        heads = pl.ds(BATCH * batch, BATCH)
        if own:
            return qkv.at[heads, pl.ds(start, size), pl.ds(HD, 2 * HD)]
        return kv0.at[heads, pl.ds(start, size), pl.ds(0, 2 * HD)]

    def spread_copy(batch, start, size, own, send_sem, recv_sem, target):
        pltpu.make_async_remote_copy(
            src_ref=cut(batch, start, size, own), dst_ref=cut(batch, start, size),
            send_sem=send_sem, recv_sem=recv_sem, device_id=(h, target), device_id_type=MESH,
        ).start()

    def push(batch, own):
        mine = pl.multiple_of(chip * 32, 32)

        @pl.loop(1, 16)
        def _(i):
            target = lax.rem(chip + i, 16)

            @pl.when(target != 0)
            def _():
                spread_copy(batch, mine, 32, own, st_s.at[batch], st_r.at[batch], 2 * target)

    def hand_over(batch, own):
        spread_copy(batch, 0, TOK, own, co_s.at[batch], co_r.at[batch], f + 1)

    def root_scatter(batch):
        @pl.when(f == 0)
        def _():
            @pl.loop(1, 16)
            def _(q):
                spread_copy(batch, pl.multiple_of(q * 32, 32), 32, True, sc_s.at[batch], sc_r.at[batch], 2 * q)

    def root_push():
        @pl.when(f == 0)
        def _():
            for batch in range(BATCHES):
                push(batch, True)
                hand_over(batch, True)
            for j in range(HPG):
                kv0[j, :, : 2 * HD] = qkv[j, :, HD : 3 * HD]

    def relay(batch):
        @pl.when((core == 0) & (f != 0))
        def _():
            arrived(cut(batch, 0, 32), sc_r.at[batch])
            push(batch, False)

    def collect(batch):
        @pl.when((core == 0) & (f != 0))
        def _():
            arrived(cut(batch, 0, 480), st_r.at[batch])
            hand_over(batch, False)

    def first_here(batch):
        @pl.when(core == 1)
        def _():
            arrived(cut(batch, 0, TOK), co_r.at[batch])

    def spread_sent(batch):
        @pl.when(f == 0)
        def _():
            arrived(cut(batch, 0, 480), sc_s.at[batch])
            arrived(cut(batch, 0, 480), st_s.at[batch])
            arrived(cut(batch, 0, TOK), co_s.at[batch])

        @pl.when((core == 0) & (f != 0))
        def _():
            arrived(cut(batch, 0, 448), st_s.at[batch])
            arrived(cut(batch, 0, TOK), co_s.at[batch])

    def send_wave(v):
        picked = jnp.concatenate(
            [qkv[j, WT * v : WT * v + WT, : 3 * HD] for j in range(HPG)], axis=0
        )
        sbuf[v] = dot(perm[...], picked).astype(BF)

        @pl.loop(1, nf)
        def _(i):
            p = lax.rem(f + i, nf)
            pltpu.make_async_remote_copy(
                src_ref=sbuf.at[v, pl.ds(pl.multiple_of(p * 16, 16), 16)],
                dst_ref=rbuf.at[v, pl.ds(pl.multiple_of(f * 16, 16), 16), pl.ds(0, 3 * HD)],
                send_sem=a2a_s.at[v], recv_sem=a2a_r.at[v], device_id=(h, p), device_id_type=MESH,
            ).start()

        own = pl.ds(pl.multiple_of(f * 16, 16), 16)
        rbuf[v, own, : 3 * HD] = sbuf[v, own]

    def attend(scores, vals):
        return dot(jnp.exp2(scores).astype(BF), vals)

    def close(total):
        return (total[:, :HD] / total[:, HD:]).astype(BF)

    def temporal(v):
        arrived(rbuf.at[v, pl.ds(0, 496), pl.ds(0, 3 * HD)], a2a_r.at[v])
        scores = dot_t(rbuf[v, :, :HD], rbuf[v, :, HD : 2 * HD])
        same = (lax.broadcasted_iota(jnp.int32, (TOK, TOK), 0) % 16) == (
            lax.broadcasted_iota(jnp.int32, (TOK, TOK), 1) % 16
        )
        weights = jnp.where(same, jnp.exp2(scores), 0.0).astype(BF)
        obuf[v] = close(dot(weights, rbuf[v, :, 2 * HD :]))

        @pl.loop(1, nf)
        def _(i):
            p = lax.rem(f + i, nf)
            pltpu.make_async_remote_copy(
                src_ref=obuf.at[v, pl.ds(pl.multiple_of(p * 16, 16), 16)],
                dst_ref=tbuf.at[v, pl.ds(pl.multiple_of(f * 16, 16), 16)],
                send_sem=ret_s.at[v], recv_sem=ret_r.at[v], device_id=(h, p), device_id_type=MESH,
            ).start()

        own = pl.ds(pl.multiple_of(f * 16, 16), 16)
        tbuf[v, own] = obuf[v, own]

    def spatial_own(j):
        at = slice(2 * HD * (j % 3), 2 * HD * (j % 3) + 2 * HD)
        raw[j // 3, :, at] = attend(dot_t(qkv[j, :, :HD], qkv[j, :, HD : 2 * HD]), qkv[j, :, 2 * HD :])

    def spatial_first(j):
        at = slice(2 * HD * (j % 3), 2 * HD * (j % 3) + 2 * HD)
        total = attend(dot_t(qkv[j, :, :HD], kv0[j, :, :HD]), kv0[j, :, HD:])
        sp[j] = close(raw[j // 3, :, at] + total)

    def copy_to(src, dst, send_sem, recv_sem, peer):
        return pltpu.make_async_remote_copy(
            src_ref=src, dst_ref=dst, send_sem=send_sem, recv_sem=recv_sem,
            device_id=(peer, f), device_id_type=MESH,
        )

    def far_copies(v):
        return [
            copy_to(
                far_s.at[v, side, :, pl.ds(WIDE * part, WIDE)], far_r.at[v, side, :, pl.ds(WIDE * part, WIDE)],
                fs_sem.at[v, side, part], fr_sem.at[v, side, part], (left, right)[side],
            )
            for part in range(2) for side in range(2)
        ]

    def near_copies(v):
        return [
            copy_to(
                near_s.at[v, side, :, pl.ds(WIDE * part, WIDE)], near_r.at[v, side, :, pl.ds(WIDE * part, WIDE)],
                ns_sem.at[v, side, part], nr_sem.at[v, side, part], (left, right)[side],
            )
            for part in range(2) for side in range(2)
        ]

    def project_out(v):
        rows = slice(WT * v, WT * v + WT)
        arrived(tbuf.at[v, pl.ds(0, 496)], ret_r.at[v])
        back = dot(unperm[...], tbuf[v])
        for j in range(HPG):
            block = back[WT * j : WT * j + WT] + sp[j, rows].astype(F32) * (1.0 - kind[j])
            att[rows, HD * j : HD * j + HD] = block.astype(BF)
        part = dot(att[rows], wo[opposite]).astype(BF)
        far_s[v, 0] = part[:HALF]
        far_s[v, 1] = part[HALF:]
        for copy in far_copies(v):
            copy.start()

    def near_terms(v):
        rows = slice(WT * v, WT * v + WT)
        near_s[v, 0] = dot(att[rows], wo[left]).astype(BF)
        near_s[v, 1] = dot(att[rows], wo[right]).astype(BF)

    def reduce_near(v):
        far = far_copies(v)
        near = near_copies(v)
        for part in range(2):
            cols = slice(WIDE * part, WIDE * part + WIDE)
            for side in range(2):
                rows = slice(HALF * side, HALF * side + HALF)
                far[2 * part + side].wait_recv()
                total = near_s[v, side, rows, cols].astype(F32) + far_r[v, side, :, cols].astype(F32)
                near_s[v, side, rows, cols] = total.astype(BF)
                near[2 * part + side].start()

    def finish(v):
        rows = slice(WT * v, WT * v + WT)
        part = dot(att[rows], wo[h]).astype(BF).astype(F32)
        for copy in near_copies(v):
            copy.wait_recv()
        out_ref[rows] = (part + near_r[v, 0].astype(F32) + near_r[v, 1].astype(F32)).astype(BF)

    loads[0].wait()
    project(0)
    project(1)
    settle(0)
    project(2)
    settle(1)
    pl.semaphore_wait(barrier, nf + 1)
    root_scatter(0)
    relay(0)
    project(3)
    settle(2)
    root_scatter(1)
    relay(1)
    settle(3)
    root_scatter(2)
    root_push()
    relay(2)
    send_wave(0)
    send_wave(1)
    for j in range(HPG):
        spatial_own(j)
    collect(0)
    collect(1)
    collect(2)
    for b in range(4):
        loads[10 + b].wait()
    send_wave(2)
    temporal(0)
    for batch in range(BATCHES):
        first_here(batch)
    for j in range(HPG):
        spatial_first(j)
    send_wave(3)
    project_out(0)
    near_terms(0)
    temporal(1)
    reduce_near(0)
    project_out(1)
    near_terms(1)
    temporal(2)
    reduce_near(1)
    project_out(2)
    near_terms(2)
    temporal(3)
    finish(0)
    reduce_near(2)
    project_out(3)
    near_terms(3)
    finish(1)
    reduce_near(3)
    finish(2)
    finish(3)

    for batch in range(BATCHES):
        spread_sent(batch)
    for v in range(WAVES):
        arrived(sbuf.at[v, pl.ds(0, 496)], a2a_s.at[v])
        arrived(obuf.at[v, pl.ds(0, 496)], ret_s.at[v])
        for copy in far_copies(v) + near_copies(v):
            copy.wait_send()


def per_device(frames_x, w_qkv, q_gain, k_gain, head_kind, w_out):
    any_spec = pl.BlockSpec(memory_space=pl.ANY)
    vmem = pl.BlockSpec(memory_space=pltpu.VMEM)
    dma = pltpu.SemaphoreType.DMA
    return pl.pallas_call(
        kernel,
        out_shape=jax.ShapeDtypeStruct((TOK, COLS), BF),
        in_specs=[pl.BlockSpec(memory_space=pltpu.SMEM), any_spec, any_spec, vmem, vmem, any_spec],
        out_specs=vmem,
        scratch_shapes=[
            pltpu.VMEM((TOK, D), BF),
            pltpu.VMEM((CHUNKS, D, 256), BF),
            pltpu.VMEM((4, HPG * HD, COLS), BF),
            pltpu.VMEM((2, TOK, 768), F32),
            pltpu.VMEM((HPG, TOK, 4 * HD), BF),
            pltpu.VMEM((HPG, TOK, 3 * HD), BF),
            pltpu.VMEM((WAVES, TOK, 3 * HD), BF),
            pltpu.VMEM((WAVES, TOK, 4 * HD), BF),
            pltpu.VMEM((WAVES, TOK, HD), BF),
            pltpu.VMEM((WAVES, TOK, HD), BF),
            pltpu.VMEM((TOK, HPG * WT), BF),
            pltpu.VMEM((HPG * WT, TOK), BF),
            pltpu.VMEM((HPG, TOK, HD), BF),
            pltpu.VMEM((TOK, HPG * HD), BF),
            pltpu.VMEM((WAVES, 2, HALF, COLS), BF),
            pltpu.VMEM((WAVES, 2, HALF, COLS), BF),
            pltpu.VMEM((WAVES, 2, WT, COLS), BF),
            pltpu.VMEM((WAVES, 2, WT, COLS), BF),
            dma((14,)),
            dma((WAVES,)),
            dma((WAVES,)),
            dma((WAVES,)),
            dma((WAVES,)),
            dma((BATCHES,)),
            dma((BATCHES,)),
            dma((BATCHES,)),
            dma((BATCHES,)),
            dma((BATCHES,)),
            dma((BATCHES,)),
            dma((WAVES, 2, 2)),
            dma((WAVES, 2, 2)),
            dma((WAVES, 2, 2)),
            dma((WAVES, 2, 2)),
        ],
        compiler_params=pltpu.CompilerParams(
            collective_id=0, has_side_effects=True, vmem_limit_bytes=60 * 1024 * 1024
        ),
    )(head_kind, frames_x, w_qkv, q_gain.reshape(1, HD), k_gain.reshape(1, HD), w_out)


def solution(mesh):
    placed = (P("frame", None), P(None, "head"), P(), P(), P("head"), P("head", None))
    return jax.shard_map(
        per_device, mesh=mesh, in_specs=placed, out_specs=P("frame", "head"), check_vma=False
    )
```

```python
import functools
import math

import jax
import jax.numpy as jnp
from jax import lax
from jax.experimental import pallas as pl
from jax.experimental.pallas import tpu as pltpu
from jax.sharding import PartitionSpec as P

MESH = pl.DeviceIdType.MESH
EPSILON = 1e-06
HPG = 6
TMAX = 4
HD = 128
TOK = 512
D = 3072
WAVES = 4
WT = TOK // WAVES
COLS = D // 4
CHUNKS = 9
SECTIONS = ((0, 1), (2, 3, 4, 5), (6, 7, 8))
STARTS = (5, 13, 17, 17)
WAITS = (0, 3, 7, 13)
HALF = WT // 2
WIDE = COLS // 2
BATCH = 2
BATCHES = HPG // BATCH
BF = jnp.bfloat16
F32 = jnp.float32


def dot(a, b):
    return jnp.dot(a, b, preferred_element_type=F32)


def dot_t(a, b):
    return lax.dot_general(a, b, (((1,), (1,)), ((), ())), preferred_element_type=F32)


def arrived(ref, sem):
    pltpu.make_async_copy(ref, ref, sem).wait()


def kernel(
    kinds, x_hbm, w_hbm, qg_ref, kg_ref, wo_hbm, out_ref,
    x, w, wo, raw, qkv, kv0, sbuf, rbuf, obuf, tbuf, perm, unperm, sp, att,
    far_s, far_r, near_s, near_r,
    load_sem, a2a_s, a2a_r, ret_s, ret_r, sc_s, sc_r, st_s, st_r, co_s, co_r, fs_sem, fr_sem, ns_sem, nr_sem,
):
    nf = 32
    h = lax.axis_index("head")
    f = lax.axis_index("frame")
    core = lax.rem(f, 2)
    chip = f // 2
    y, z = chip // 4, lax.rem(chip, 4)
    left, right, opposite = lax.rem(h + 3, 4), lax.rem(h + 1, 4), lax.rem(h + 2, 4)

    barrier = pltpu.get_barrier_semaphore()

    @pl.loop(1, nf)
    def _(i):
        pl.semaphore_signal(barrier, inc=1, device_id=(h, lax.rem(f + i, nf)), device_id_type=MESH)

    for peer in (left, right):
        pl.semaphore_signal(barrier, inc=1, device_id=(peer, f), device_id_type=MESH)

    sources = [(x_hbm, x)]
    for j in range(HPG):
        sources.append((w_hbm.at[:, pl.ds(3 * HD * j + HD, 2 * HD)], w.at[j]))
    for j in range(HPG):
        sources.append(
            (w_hbm.at[:, pl.ds(3 * HD * j, HD)], w.at[HPG + j // 2, :, pl.ds(HD * (j % 2), HD)])
        )
    for b in range(4):
        sources.append((wo_hbm.at[:, pl.ds(COLS * b, COLS)], wo.at[b]))
    loads = [
        pltpu.make_async_copy(source, target, load_sem.at[i])
        for i, (source, target) in enumerate(sources)
    ]
    for load in loads[: STARTS[0]]:
        load.start()

    kind = [kinds[j] for j in range(HPG)]
    count = sum(kind)
    holds = [[None] * HPG for _ in range(TMAX)]
    before = jnp.int32(0)
    for j in range(HPG):
        rank = kind[j] * before + (1 - kind[j]) * (count + j - before)
        for t in range(TMAX):
            holds[t][j] = (1 - jnp.minimum((rank - t) * (rank - t), 1)).astype(F32)
        before = before + kind[j]
    kind = [val.astype(F32) for val in kind]

    def spread(shape, mixed_dim):
        mixed = lax.broadcasted_iota(jnp.int32, shape, mixed_dim)
        token = lax.broadcasted_iota(jnp.int32, shape, 1 - mixed_dim)
        same = ((mixed // 16) * 4 + mixed % 4 == token).astype(F32)
        slot = (mixed // 4) % 4
        return [jnp.where(slot == t, same, 0.0) for t in range(TMAX)]

    slots = spread((TOK, WT), 0)
    for j in range(HPG):
        perm[:, WT * j : WT * j + WT] = sum(slots[t] * holds[t][j] for t in range(TMAX)).astype(BF)
    slots = spread((WT, TOK), 1)
    for j in range(HPG):
        total = sum(slots[t] * (holds[t][j] * kind[j]) for t in range(TMAX))
        unperm[WT * j : WT * j + WT] = total.astype(BF)
    for j in range(HPG):
        qkv[j, :, 3 * HD :] = jnp.ones((TOK, HD), BF)
        kv0[j, :, 2 * HD :] = jnp.ones((TOK, HD), BF)
    for v in range(WAVES):
        rbuf[v, :, 3 * HD :] = jnp.ones((TOK, HD), BF)

    q_gain = qg_ref[...] * (math.log2(math.e) / math.sqrt(HD))
    k_gain = kg_ref[...]

    def norm(val, gain):
        mean_square = jnp.mean(val * val, axis=-1, keepdims=True)
        return (val * lax.rsqrt(mean_square + EPSILON) * gain).astype(BF)

    def project(number):
        for load in loads[WAITS[number] : WAITS[number + 1]]:
            load.wait()
        for load in loads[STARTS[number] : STARTS[number + 1]]:
            load.start()
        for c in SECTIONS[number]:
            val = dot(x[...], w[c])
            one, two = val[:, :HD], val[:, HD:]
            if c < HPG:
                qkv[c, :, HD : 2 * HD] = norm(one, k_gain)
                qkv[c, :, 2 * HD : 3 * HD] = two.astype(BF)
            else:
                qkv[2 * (c - HPG), :, :HD] = norm(one, q_gain)
                qkv[2 * (c - HPG) + 1, :, :HD] = norm(two, q_gain)

    def cut(head, n, start, size, own=False):
        heads = pl.ds(head, n)
        if own:
            return qkv.at[heads, pl.ds(start, size), pl.ds(HD, 2 * HD)]
        return kv0.at[heads, pl.ds(start, size), pl.ds(0, 2 * HD)]

    def spread_copy(head, n, start, size, own, send_sem, recv_sem, target):
        pltpu.make_async_remote_copy(
            src_ref=cut(head, n, start, size, own), dst_ref=cut(head, n, start, size),
            send_sem=send_sem, recv_sem=recv_sem, device_id=(h, target), device_id_type=MESH,
        ).start()

    def push(batch, number, own):
        for side in range(2):
            major, minor = ((y, z), (z, y))[side]
            if number == 0:
                start, size = pl.multiple_of((major * 4 + minor) * 32, 32), 32
            else:
                start, size = pl.multiple_of(major * 128, 128), 128
            for i in range(1, 4):
                if side == number:
                    target = (y * 4 + lax.rem(z + i, 4)) * 2
                else:
                    target = (lax.rem(y + i, 4) * 4 + z) * 2

                @pl.when(target != 0)
                def _():
                    spread_copy(
                        BATCH * batch + side, 1, start, size, own,
                        st_s.at[batch, number], st_r.at[batch, number], target,
                    )

    def hand_over(batch, own):
        spread_copy(BATCH * batch, BATCH, 0, TOK, own, co_s.at[batch], co_r.at[batch], f + 1)

    def root_scatter(batch):
        @pl.when(f == 0)
        def _():
            @pl.loop(1, 16)
            def _(q):
                start = pl.multiple_of(q * 32, 32)
                for side in range(2):
                    target = 2 * q if side == 0 else (lax.rem(q, 4) * 4 + q // 4) * 2
                    spread_copy(BATCH * batch + side, 1, start, 32, True, sc_s.at[batch], sc_r.at[batch], target)

    def root_push():
        @pl.when(f == 0)
        def _():
            for batch in range(BATCHES):
                push(batch, 0, True)
                push(batch, 1, True)
                hand_over(batch, True)
            for j in range(HPG):
                kv0[j, :, : 2 * HD] = qkv[j, :, HD : 3 * HD]

    def whole(batch, size):
        return cut(BATCH * batch, BATCH, 0, size)

    def relay(batch, number):
        @pl.when((core == 0) & (f != 0))
        def _():
            if number == 0:
                arrived(whole(batch, 32), sc_r.at[batch])
            else:
                arrived(whole(batch, 96), st_r.at[batch, 0])
            push(batch, number, False)

    def collect(batch):
        @pl.when((core == 0) & (f != 0))
        def _():
            arrived(whole(batch, 384), st_r.at[batch, 1])
            hand_over(batch, False)

    def first_here(batch):
        @pl.when(core == 1)
        def _():
            arrived(whole(batch, TOK), co_r.at[batch])

    def spread_sent(batch):
        on_line = (chip != 0) & ((y == 0) | (z == 0))

        @pl.when(f == 0)
        def _():
            arrived(whole(batch, 480), sc_s.at[batch])

        @pl.when((core == 0) & on_line)
        def _():
            arrived(whole(batch, 80), st_s.at[batch, 0])
            arrived(whole(batch, 320), st_s.at[batch, 1])

        @pl.when((core == 0) & jnp.logical_not(on_line))
        def _():
            arrived(whole(batch, 96), st_s.at[batch, 0])
            arrived(whole(batch, 384), st_s.at[batch, 1])

        @pl.when(core == 0)
        def _():
            arrived(whole(batch, TOK), co_s.at[batch])

    def send_wave(v):
        picked = jnp.concatenate(
            [qkv[j, WT * v : WT * v + WT, : 3 * HD] for j in range(HPG)], axis=0
        )
        sbuf[v] = dot(perm[...], picked).astype(BF)

        @pl.loop(1, nf)
        def _(i):
            p = lax.rem(f + i, nf)
            pltpu.make_async_remote_copy(
                src_ref=sbuf.at[v, pl.ds(pl.multiple_of(p * 16, 16), 16)],
                dst_ref=rbuf.at[v, pl.ds(pl.multiple_of(f * 16, 16), 16), pl.ds(0, 3 * HD)],
                send_sem=a2a_s.at[v], recv_sem=a2a_r.at[v], device_id=(h, p), device_id_type=MESH,
            ).start()

        own = pl.ds(pl.multiple_of(f * 16, 16), 16)
        rbuf[v, own, : 3 * HD] = sbuf[v, own]

    def attend(scores, vals):
        return dot(jnp.exp2(scores).astype(BF), vals)

    def close(total):
        return (total[:, :HD] / total[:, HD:]).astype(BF)

    def temporal(v):
        arrived(rbuf.at[v, pl.ds(0, 496), pl.ds(0, 3 * HD)], a2a_r.at[v])
        scores = dot_t(rbuf[v, :, :HD], rbuf[v, :, HD : 2 * HD])
        same = (lax.broadcasted_iota(jnp.int32, (TOK, TOK), 0) % 16) == (
            lax.broadcasted_iota(jnp.int32, (TOK, TOK), 1) % 16
        )
        weights = jnp.where(same, jnp.exp2(scores), 0.0).astype(BF)
        obuf[v] = close(dot(weights, rbuf[v, :, 2 * HD :]))

        @pl.loop(1, nf)
        def _(i):
            p = lax.rem(f + i, nf)
            pltpu.make_async_remote_copy(
                src_ref=obuf.at[v, pl.ds(pl.multiple_of(p * 16, 16), 16)],
                dst_ref=tbuf.at[v, pl.ds(pl.multiple_of(f * 16, 16), 16)],
                send_sem=ret_s.at[v], recv_sem=ret_r.at[v], device_id=(h, p), device_id_type=MESH,
            ).start()

        own = pl.ds(pl.multiple_of(f * 16, 16), 16)
        tbuf[v, own] = obuf[v, own]

    def spatial_own(j):
        at = slice(2 * HD * (j % 3), 2 * HD * (j % 3) + 2 * HD)
        raw[j // 3, :, at] = attend(dot_t(qkv[j, :, :HD], qkv[j, :, HD : 2 * HD]), qkv[j, :, 2 * HD :])

    def spatial_first(j):
        at = slice(2 * HD * (j % 3), 2 * HD * (j % 3) + 2 * HD)
        total = attend(dot_t(qkv[j, :, :HD], kv0[j, :, :HD]), kv0[j, :, HD:])
        sp[j] = close(raw[j // 3, :, at] + total)

    def copy_to(src, dst, send_sem, recv_sem, peer):
        return pltpu.make_async_remote_copy(
            src_ref=src, dst_ref=dst, send_sem=send_sem, recv_sem=recv_sem,
            device_id=(peer, f), device_id_type=MESH,
        )

    def far_copies(v):
        return [
            copy_to(
                far_s.at[v, side, :, pl.ds(WIDE * part, WIDE)], far_r.at[v, side, :, pl.ds(WIDE * part, WIDE)],
                fs_sem.at[v, side, part], fr_sem.at[v, side, part], (left, right)[side],
            )
            for part in range(2) for side in range(2)
        ]

    def near_copies(v):
        return [
            copy_to(
                near_s.at[v, side, :, pl.ds(WIDE * part, WIDE)], near_r.at[v, side, :, pl.ds(WIDE * part, WIDE)],
                ns_sem.at[v, side, part], nr_sem.at[v, side, part], (left, right)[side],
            )
            for part in range(2) for side in range(2)
        ]

    def project_out(v):
        rows = slice(WT * v, WT * v + WT)
        arrived(tbuf.at[v, pl.ds(0, 496)], ret_r.at[v])
        back = dot(unperm[...], tbuf[v])
        for j in range(HPG):
            block = back[WT * j : WT * j + WT] + sp[j, rows].astype(F32) * (1.0 - kind[j])
            att[rows, HD * j : HD * j + HD] = block.astype(BF)
        part = dot(att[rows], wo[opposite]).astype(BF)
        far_s[v, 0] = part[:HALF]
        far_s[v, 1] = part[HALF:]
        for copy in far_copies(v):
            copy.start()

    def near_terms(v):
        rows = slice(WT * v, WT * v + WT)
        near_s[v, 0] = dot(att[rows], wo[left]).astype(BF)
        near_s[v, 1] = dot(att[rows], wo[right]).astype(BF)

    def reduce_near(v):
        far = far_copies(v)
        near = near_copies(v)
        for part in range(2):
            cols = slice(WIDE * part, WIDE * part + WIDE)
            for side in range(2):
                rows = slice(HALF * side, HALF * side + HALF)
                far[2 * part + side].wait_recv()
                total = near_s[v, side, rows, cols].astype(F32) + far_r[v, side, :, cols].astype(F32)
                near_s[v, side, rows, cols] = total.astype(BF)
                near[2 * part + side].start()

    def finish(v):
        rows = slice(WT * v, WT * v + WT)
        part = dot(att[rows], wo[h]).astype(BF).astype(F32)
        for copy in near_copies(v):
            copy.wait_recv()
        out_ref[rows] = (part + near_r[v, 0].astype(F32) + near_r[v, 1].astype(F32)).astype(BF)

    project(0)
    project(1)
    pl.semaphore_wait(barrier, nf + 1)
    for batch in range(BATCHES):
        root_scatter(batch)
    root_push()
    relay(0, 0)
    project(2)
    relay(1, 0)
    relay(0, 1)
    relay(2, 0)
    send_wave(0)
    for j in range(3):
        spatial_own(j)
    relay(1, 1)
    relay(2, 1)
    for j in range(3, HPG):
        spatial_own(j)
    collect(0)
    temporal(0)
    collect(1)
    collect(2)
    send_wave(1)
    for b in range(4):
        loads[13 + b].wait()
    for batch in range(BATCHES):
        first_here(batch)
        for j in range(BATCH * batch, BATCH * batch + BATCH):
            spatial_first(j)
    project_out(0)
    near_terms(0)
    temporal(1)
    send_wave(2)
    reduce_near(0)
    project_out(1)
    near_terms(1)
    temporal(2)
    send_wave(3)
    reduce_near(1)
    project_out(2)
    near_terms(2)
    temporal(3)
    finish(0)
    reduce_near(2)
    project_out(3)
    near_terms(3)
    finish(1)
    reduce_near(3)
    finish(2)
    finish(3)

    for batch in range(BATCHES):
        spread_sent(batch)
    for v in range(WAVES):
        arrived(sbuf.at[v, pl.ds(0, 496)], a2a_s.at[v])
        arrived(obuf.at[v, pl.ds(0, 496)], ret_s.at[v])
        for copy in far_copies(v) + near_copies(v):
            copy.wait_send()


def per_device(frames_x, w_qkv, q_gain, k_gain, head_kind, w_out):
    any_spec = pl.BlockSpec(memory_space=pl.ANY)
    vmem = pl.BlockSpec(memory_space=pltpu.VMEM)
    dma = pltpu.SemaphoreType.DMA
    return pl.pallas_call(
        kernel,
        out_shape=jax.ShapeDtypeStruct((TOK, COLS), BF),
        in_specs=[pl.BlockSpec(memory_space=pltpu.SMEM), any_spec, any_spec, vmem, vmem, any_spec],
        out_specs=vmem,
        scratch_shapes=[
            pltpu.VMEM((TOK, D), BF),
            pltpu.VMEM((CHUNKS, D, 256), BF),
            pltpu.VMEM((4, HPG * HD, COLS), BF),
            pltpu.VMEM((2, TOK, 768), F32),
            pltpu.VMEM((HPG, TOK, 4 * HD), BF),
            pltpu.VMEM((HPG, TOK, 3 * HD), BF),
            pltpu.VMEM((WAVES, TOK, 3 * HD), BF),
            pltpu.VMEM((WAVES, TOK, 4 * HD), BF),
            pltpu.VMEM((WAVES, TOK, HD), BF),
            pltpu.VMEM((WAVES, TOK, HD), BF),
            pltpu.VMEM((TOK, HPG * WT), BF),
            pltpu.VMEM((HPG * WT, TOK), BF),
            pltpu.VMEM((HPG, TOK, HD), BF),
            pltpu.VMEM((TOK, HPG * HD), BF),
            pltpu.VMEM((WAVES, 2, HALF, COLS), BF),
            pltpu.VMEM((WAVES, 2, HALF, COLS), BF),
            pltpu.VMEM((WAVES, 2, WT, COLS), BF),
            pltpu.VMEM((WAVES, 2, WT, COLS), BF),
            dma((17,)),
            dma((WAVES,)),
            dma((WAVES,)),
            dma((WAVES,)),
            dma((WAVES,)),
            dma((BATCHES,)),
            dma((BATCHES,)),
            dma((BATCHES, 2)),
            dma((BATCHES, 2)),
            dma((BATCHES,)),
            dma((BATCHES,)),
            dma((WAVES, 2, 2)),
            dma((WAVES, 2, 2)),
            dma((WAVES, 2, 2)),
            dma((WAVES, 2, 2)),
        ],
        compiler_params=pltpu.CompilerParams(
            collective_id=0, has_side_effects=True, vmem_limit_bytes=60 * 1024 * 1024
        ),
    )(head_kind, frames_x, w_qkv, q_gain.reshape(1, HD), k_gain.reshape(1, HD), w_out)


def solution(mesh):
    placed = (P("frame", None), P(None, "head"), P(), P(), P("head"), P("head", None))
    return jax.shard_map(
        per_device, mesh=mesh, in_specs=placed, out_specs=P("frame", "head"), check_vma=False
    )
```

```python
import functools
import math

import jax
import jax.numpy as jnp
from jax import lax
from jax.experimental import pallas as pl
from jax.experimental.pallas import tpu as pltpu
from jax.sharding import PartitionSpec as P

MESH = pl.DeviceIdType.MESH
EPSILON = 1e-06
HPG = 6
TMAX = 4
HD = 128
TOK = 512
D = 3072
WAVES = 4
WT = TOK // WAVES
COLS = D // 4
CHUNKS = 9
SECTIONS = ((0, 1), (2, 3, 4, 5), (6, 7, 8))
STARTS = (5, 13, 17, 17)
WAITS = (0, 3, 7, 13)
HALF = WT // 2
WIDE = COLS // 2
BATCH = 2
BATCHES = HPG // BATCH
BF = jnp.bfloat16
F32 = jnp.float32


def dot(a, b):
    return jnp.dot(a, b, preferred_element_type=F32)


def dot_t(a, b):
    return lax.dot_general(a, b, (((1,), (1,)), ((), ())), preferred_element_type=F32)


def arrived(ref, sem):
    pltpu.make_async_copy(ref, ref, sem).wait()


def kernel(
    kinds, x_hbm, w_hbm, qg_ref, kg_ref, wo_hbm, out_hbm,
    x, w, wo, raw, qkv, kv0, sbuf, rbuf, obuf, tbuf, perm, unperm, sp, att,
    far_s, far_r, near_s, near_r, out_ref,
    load_sem, a2a_s, a2a_r, ret_s, ret_r, sc_s, sc_r, st_s, st_r, co_s, co_r, fs_sem, fr_sem, ns_sem, nr_sem, out_sem,
):
    nf = 32
    h = lax.axis_index("head")
    f = lax.axis_index("frame")
    core = lax.rem(f, 2)
    chip = f // 2
    y, z = chip // 4, lax.rem(chip, 4)
    left, right, opposite = lax.rem(h + 3, 4), lax.rem(h + 1, 4), lax.rem(h + 2, 4)

    barrier = pltpu.get_barrier_semaphore()

    @pl.loop(1, nf)
    def _(i):
        pl.semaphore_signal(barrier, inc=1, device_id=(h, lax.rem(f + i, nf)), device_id_type=MESH)

    for peer in (left, right):
        pl.semaphore_signal(barrier, inc=1, device_id=(peer, f), device_id_type=MESH)

    sources = [(x_hbm, x)]
    for j in range(HPG):
        sources.append((w_hbm.at[:, pl.ds(3 * HD * j + HD, 2 * HD)], w.at[j]))
    for j in range(HPG):
        sources.append(
            (w_hbm.at[:, pl.ds(3 * HD * j, HD)], w.at[HPG + j // 2, :, pl.ds(HD * (j % 2), HD)])
        )
    for b in range(4):
        sources.append((wo_hbm.at[:, pl.ds(COLS * b, COLS)], wo.at[b]))
    loads = [
        pltpu.make_async_copy(source, target, load_sem.at[i])
        for i, (source, target) in enumerate(sources)
    ]
    for load in loads[: STARTS[0]]:
        load.start()

    kind = [kinds[j] for j in range(HPG)]
    count = sum(kind)
    holds = [[None] * HPG for _ in range(TMAX)]
    before = jnp.int32(0)
    for j in range(HPG):
        rank = kind[j] * before + (1 - kind[j]) * (count + j - before)
        for t in range(TMAX):
            holds[t][j] = (1 - jnp.minimum((rank - t) * (rank - t), 1)).astype(F32)
        before = before + kind[j]
    kind = [val.astype(F32) for val in kind]

    def spread(shape, mixed_dim):
        mixed = lax.broadcasted_iota(jnp.int32, shape, mixed_dim)
        token = lax.broadcasted_iota(jnp.int32, shape, 1 - mixed_dim)
        same = ((mixed // 16) * 4 + mixed % 4 == token).astype(F32)
        slot = (mixed // 4) % 4
        return [jnp.where(slot == t, same, 0.0) for t in range(TMAX)]

    slots = spread((TOK, WT), 0)
    for j in range(HPG):
        perm[:, WT * j : WT * j + WT] = sum(slots[t] * holds[t][j] for t in range(TMAX)).astype(BF)
    slots = spread((WT, TOK), 1)
    for j in range(HPG):
        total = sum(slots[t] * (holds[t][j] * kind[j]) for t in range(TMAX))
        unperm[WT * j : WT * j + WT] = total.astype(BF)
    for j in range(HPG):
        qkv[j, :, 3 * HD :] = jnp.ones((TOK, HD), BF)
        kv0[j, :, 2 * HD :] = jnp.ones((TOK, HD), BF)
    for v in range(WAVES):
        rbuf[v, :, 3 * HD :] = jnp.ones((TOK, HD), BF)

    q_gain = qg_ref[...] * (math.log2(math.e) / math.sqrt(HD))
    k_gain = kg_ref[...]

    def norm(val, gain):
        mean_square = jnp.mean(val * val, axis=-1, keepdims=True)
        return (val * lax.rsqrt(mean_square + EPSILON) * gain).astype(BF)

    def project(number):
        for load in loads[WAITS[number] : WAITS[number + 1]]:
            load.wait()
        for load in loads[STARTS[number] : STARTS[number + 1]]:
            load.start()
        for c in SECTIONS[number]:
            val = dot(x[...], w[c])
            one, two = val[:, :HD], val[:, HD:]
            if c < HPG:
                qkv[c, :, HD : 2 * HD] = norm(one, k_gain)
                qkv[c, :, 2 * HD : 3 * HD] = two.astype(BF)
            else:
                qkv[2 * (c - HPG), :, :HD] = norm(one, q_gain)
                qkv[2 * (c - HPG) + 1, :, :HD] = norm(two, q_gain)

    def cut(head, n, start, size, own=False):
        heads = pl.ds(head, n)
        if own:
            return qkv.at[heads, pl.ds(start, size), pl.ds(HD, 2 * HD)]
        return kv0.at[heads, pl.ds(start, size), pl.ds(0, 2 * HD)]

    def spread_copy(head, n, start, size, own, send_sem, recv_sem, target):
        pltpu.make_async_remote_copy(
            src_ref=cut(head, n, start, size, own), dst_ref=cut(head, n, start, size),
            send_sem=send_sem, recv_sem=recv_sem, device_id=(h, target), device_id_type=MESH,
        ).start()

    def push(batch, number, own):
        for side in range(2):
            major, minor = ((y, z), (z, y))[side]
            if number == 0:
                start, size = pl.multiple_of((major * 4 + minor) * 32, 32), 32
            else:
                start, size = pl.multiple_of(major * 128, 128), 128
            for i in range(1, 4):
                if side == number:
                    target = (y * 4 + lax.rem(z + i, 4)) * 2
                else:
                    target = (lax.rem(y + i, 4) * 4 + z) * 2

                @pl.when(target != 0)
                def _():
                    spread_copy(
                        BATCH * batch + side, 1, start, size, own,
                        st_s.at[batch, number], st_r.at[batch, number], target,
                    )

    def hand_over(batch, own):
        spread_copy(BATCH * batch, BATCH, 0, TOK, own, co_s.at[batch], co_r.at[batch], f + 1)

    def root_scatter(batch):
        @pl.when(f == 0)
        def _():
            @pl.loop(1, 16)
            def _(q):
                start = pl.multiple_of(q * 32, 32)
                for side in range(2):
                    target = 2 * q if side == 0 else (lax.rem(q, 4) * 4 + q // 4) * 2
                    spread_copy(BATCH * batch + side, 1, start, 32, True, sc_s.at[batch], sc_r.at[batch], target)

    def root_push():
        @pl.when(f == 0)
        def _():
            for batch in range(BATCHES):
                push(batch, 0, True)
                push(batch, 1, True)
                hand_over(batch, True)
            for j in range(HPG):
                kv0[j, :, : 2 * HD] = qkv[j, :, HD : 3 * HD]

    def whole(batch, size):
        return cut(BATCH * batch, BATCH, 0, size)

    def relay(batch, number):
        @pl.when((core == 0) & (f != 0))
        def _():
            if number == 0:
                arrived(whole(batch, 32), sc_r.at[batch])
            else:
                arrived(whole(batch, 96), st_r.at[batch, 0])
            push(batch, number, False)

    def collect(batch):
        @pl.when((core == 0) & (f != 0))
        def _():
            arrived(whole(batch, 384), st_r.at[batch, 1])
            hand_over(batch, False)

    def first_here(batch):
        @pl.when(core == 1)
        def _():
            arrived(whole(batch, TOK), co_r.at[batch])

    def spread_sent(batch):
        on_line = (chip != 0) & ((y == 0) | (z == 0))

        @pl.when(f == 0)
        def _():
            arrived(whole(batch, 480), sc_s.at[batch])

        @pl.when((core == 0) & on_line)
        def _():
            arrived(whole(batch, 80), st_s.at[batch, 0])
            arrived(whole(batch, 320), st_s.at[batch, 1])

        @pl.when((core == 0) & jnp.logical_not(on_line))
        def _():
            arrived(whole(batch, 96), st_s.at[batch, 0])
            arrived(whole(batch, 384), st_s.at[batch, 1])

        @pl.when(core == 0)
        def _():
            arrived(whole(batch, TOK), co_s.at[batch])

    def send_wave(v):
        picked = jnp.concatenate(
            [qkv[j, WT * v : WT * v + WT, : 3 * HD] for j in range(HPG)], axis=0
        )
        sbuf[v] = dot(perm[...], picked).astype(BF)

        @pl.loop(1, nf)
        def _(i):
            p = lax.rem(f + i, nf)
            pltpu.make_async_remote_copy(
                src_ref=sbuf.at[v, pl.ds(pl.multiple_of(p * 16, 16), 16)],
                dst_ref=rbuf.at[v, pl.ds(pl.multiple_of(f * 16, 16), 16), pl.ds(0, 3 * HD)],
                send_sem=a2a_s.at[v], recv_sem=a2a_r.at[v], device_id=(h, p), device_id_type=MESH,
            ).start()

        own = pl.ds(pl.multiple_of(f * 16, 16), 16)
        rbuf[v, own, : 3 * HD] = sbuf[v, own]

    def attend(scores, vals):
        return dot(jnp.exp2(scores).astype(BF), vals)

    def close(total):
        return (total[:, :HD] / total[:, HD:]).astype(BF)

    def temporal(v):
        arrived(rbuf.at[v, pl.ds(0, 496), pl.ds(0, 3 * HD)], a2a_r.at[v])
        scores = dot_t(rbuf[v, :, :HD], rbuf[v, :, HD : 2 * HD])
        same = (lax.broadcasted_iota(jnp.int32, (TOK, TOK), 0) % 16) == (
            lax.broadcasted_iota(jnp.int32, (TOK, TOK), 1) % 16
        )
        weights = jnp.where(same, jnp.exp2(scores), 0.0).astype(BF)
        obuf[v] = close(dot(weights, rbuf[v, :, 2 * HD :]))

        @pl.loop(1, nf)
        def _(i):
            p = lax.rem(f + i, nf)
            pltpu.make_async_remote_copy(
                src_ref=obuf.at[v, pl.ds(pl.multiple_of(p * 16, 16), 16)],
                dst_ref=tbuf.at[v, pl.ds(pl.multiple_of(f * 16, 16), 16)],
                send_sem=ret_s.at[v], recv_sem=ret_r.at[v], device_id=(h, p), device_id_type=MESH,
            ).start()

        own = pl.ds(pl.multiple_of(f * 16, 16), 16)
        tbuf[v, own] = obuf[v, own]

    def spatial_own(j):
        at = slice(2 * HD * (j % 3), 2 * HD * (j % 3) + 2 * HD)
        raw[j // 3, :, at] = attend(dot_t(qkv[j, :, :HD], qkv[j, :, HD : 2 * HD]), qkv[j, :, 2 * HD :])

    def spatial_first(j):
        at = slice(2 * HD * (j % 3), 2 * HD * (j % 3) + 2 * HD)
        total = attend(dot_t(qkv[j, :, :HD], kv0[j, :, :HD]), kv0[j, :, HD:])
        sp[j] = close(raw[j // 3, :, at] + total)

    def copy_to(src, dst, send_sem, recv_sem, peer):
        return pltpu.make_async_remote_copy(
            src_ref=src, dst_ref=dst, send_sem=send_sem, recv_sem=recv_sem,
            device_id=(peer, f), device_id_type=MESH,
        )

    def far_copies(v):
        return [
            copy_to(
                far_s.at[v, side, :, pl.ds(WIDE * part, WIDE)], far_r.at[v, side, :, pl.ds(WIDE * part, WIDE)],
                fs_sem.at[v, side, part], fr_sem.at[v, side, part], (left, right)[side],
            )
            for part in range(2) for side in range(2)
        ]

    def near_copies(v):
        return [
            copy_to(
                near_s.at[v, side, :, pl.ds(WIDE * part, WIDE)], near_r.at[v, side, :, pl.ds(WIDE * part, WIDE)],
                ns_sem.at[v, side, part], nr_sem.at[v, side, part], (left, right)[side],
            )
            for part in range(2) for side in range(2)
        ]

    def project_out(v):
        rows = slice(WT * v, WT * v + WT)
        arrived(tbuf.at[v, pl.ds(0, 496)], ret_r.at[v])
        back = dot(unperm[...], tbuf[v])
        for j in range(HPG):
            block = back[WT * j : WT * j + WT] + sp[j, rows].astype(F32) * (1.0 - kind[j])
            att[rows, HD * j : HD * j + HD] = block.astype(BF)
        part = dot(att[rows], wo[opposite]).astype(BF)
        far_s[v, 0] = part[:HALF]
        far_s[v, 1] = part[HALF:]
        for copy in far_copies(v):
            copy.start()

    def near_terms(v):
        rows = slice(WT * v, WT * v + WT)
        near_s[v, 0] = dot(att[rows], wo[left]).astype(BF)
        near_s[v, 1] = dot(att[rows], wo[right]).astype(BF)

    def reduce_near(v):
        far = far_copies(v)
        near = near_copies(v)
        for part in range(2):
            cols = slice(WIDE * part, WIDE * part + WIDE)
            for side in range(2):
                rows = slice(HALF * side, HALF * side + HALF)
                far[2 * part + side].wait_recv()
                total = near_s[v, side, rows, cols].astype(F32) + far_r[v, side, :, cols].astype(F32)
                near_s[v, side, rows, cols] = total.astype(BF)
                near[2 * part + side].start()

    def out_copy(v):
        rows = pl.ds(WT * v, WT)
        return pltpu.make_async_copy(out_ref.at[rows], out_hbm.at[rows], out_sem.at[v])

    def finish(v):
        rows = slice(WT * v, WT * v + WT)
        part = dot(att[rows], wo[h]).astype(BF).astype(F32)
        for copy in near_copies(v):
            copy.wait_recv()
        out_ref[rows] = (part + near_r[v, 0].astype(F32) + near_r[v, 1].astype(F32)).astype(BF)
        out_copy(v).start()

    project(0)
    project(1)
    pl.semaphore_wait(barrier, nf + 1)
    for batch in range(BATCHES):
        root_scatter(batch)
    root_push()
    relay(0, 0)
    project(2)
    relay(1, 0)
    relay(0, 1)
    relay(2, 0)
    send_wave(0)
    for j in range(3):
        spatial_own(j)
    relay(1, 1)
    relay(2, 1)
    for j in range(3, HPG):
        spatial_own(j)
    collect(0)
    temporal(0)
    collect(1)
    collect(2)
    send_wave(1)
    for b in range(4):
        loads[13 + b].wait()
    for batch in range(BATCHES):
        first_here(batch)
        for j in range(BATCH * batch, BATCH * batch + BATCH):
            spatial_first(j)
    project_out(0)
    near_terms(0)
    temporal(1)
    send_wave(2)
    reduce_near(0)
    project_out(1)
    near_terms(1)
    temporal(2)
    send_wave(3)
    reduce_near(1)
    project_out(2)
    near_terms(2)
    temporal(3)
    finish(0)
    reduce_near(2)
    project_out(3)
    near_terms(3)
    finish(1)
    reduce_near(3)
    finish(2)
    finish(3)

    for batch in range(BATCHES):
        spread_sent(batch)
    for v in range(WAVES):
        out_copy(v).wait()
        arrived(sbuf.at[v, pl.ds(0, 496)], a2a_s.at[v])
        arrived(obuf.at[v, pl.ds(0, 496)], ret_s.at[v])
        for copy in far_copies(v) + near_copies(v):
            copy.wait_send()


def per_device(frames_x, w_qkv, q_gain, k_gain, head_kind, w_out):
    any_spec = pl.BlockSpec(memory_space=pl.ANY)
    vmem = pl.BlockSpec(memory_space=pltpu.VMEM)
    dma = pltpu.SemaphoreType.DMA
    return pl.pallas_call(
        kernel,
        out_shape=jax.ShapeDtypeStruct((TOK, COLS), BF),
        in_specs=[pl.BlockSpec(memory_space=pltpu.SMEM), any_spec, any_spec, vmem, vmem, any_spec],
        out_specs=any_spec,
        scratch_shapes=[
            pltpu.VMEM((TOK, D), BF),
            pltpu.VMEM((CHUNKS, D, 256), BF),
            pltpu.VMEM((4, HPG * HD, COLS), BF),
            pltpu.VMEM((2, TOK, 768), F32),
            pltpu.VMEM((HPG, TOK, 4 * HD), BF),
            pltpu.VMEM((HPG, TOK, 3 * HD), BF),
            pltpu.VMEM((WAVES, TOK, 3 * HD), BF),
            pltpu.VMEM((WAVES, TOK, 4 * HD), BF),
            pltpu.VMEM((WAVES, TOK, HD), BF),
            pltpu.VMEM((WAVES, TOK, HD), BF),
            pltpu.VMEM((TOK, HPG * WT), BF),
            pltpu.VMEM((HPG * WT, TOK), BF),
            pltpu.VMEM((HPG, TOK, HD), BF),
            pltpu.VMEM((TOK, HPG * HD), BF),
            pltpu.VMEM((WAVES, 2, HALF, COLS), BF),
            pltpu.VMEM((WAVES, 2, HALF, COLS), BF),
            pltpu.VMEM((WAVES, 2, WT, COLS), BF),
            pltpu.VMEM((WAVES, 2, WT, COLS), BF),
            pltpu.VMEM((TOK, COLS), BF),
            dma((17,)),
            dma((WAVES,)),
            dma((WAVES,)),
            dma((WAVES,)),
            dma((WAVES,)),
            dma((BATCHES,)),
            dma((BATCHES,)),
            dma((BATCHES, 2)),
            dma((BATCHES, 2)),
            dma((BATCHES,)),
            dma((BATCHES,)),
            dma((WAVES, 2, 2)),
            dma((WAVES, 2, 2)),
            dma((WAVES, 2, 2)),
            dma((WAVES, 2, 2)),
            dma((WAVES,)),
        ],
        compiler_params=pltpu.CompilerParams(
            collective_id=0, has_side_effects=True, vmem_limit_bytes=60 * 1024 * 1024
        ),
    )(head_kind, frames_x, w_qkv, q_gain.reshape(1, HD), k_gain.reshape(1, HD), w_out)


def solution(mesh):
    placed = (P("frame", None), P(None, "head"), P(), P(), P("head"), P("head", None))
    return jax.shard_map(
        per_device, mesh=mesh, in_specs=placed, out_specs=P("frame", "head"), check_vma=False
    )
```
